32 devices in a mesh: dp: 8 (over y, x, core), centre: 4 (over z).
Axes of the slice: x: 2, y: 2, z: 4, core: 2. Of those that a mesh axis runs over, the one named last changes fastest.
Arguments:
- points: float32 [9, 65536], P(None, 'dp'), may hold values from -6 to 6
- centres: float32 [9, 16384], P(None, 'centre'), may hold values from -6 to 6
- t_inverse: float32 [16384, 16384], P('dp', 'centre'), as said below
- a_inverse: float32 [16384, 16384], P('dp', 'centre'), as said below
- solution: float32 [16384], P('centre'), may hold values from -6 to 6
- residual: float32 [16384], P('centre'), may hold values from -6 to 6
- direction: float32 [16384], P('centre'), may hold values from -6 to 6
Outputs:
- new_solution: float32 [16384], P('centre')
- new_residual: float32 [16384], P('centre')
- new_direction: float32 [16384], P('centre')
The draws below stay inside these ranges and needn't reach their ends.
Inputs may be any that keep to these rules, and one draw needn't show every extreme that they name: t_inverse and a_inverse are upper triangular: zero below the diagonal, positive on it. `a_inverse`: upper triangular: zero below the diagonal, positive on it.
All inputs are finite; a program needn't handle non-finite values.
Results may differ from the reference program's by a relative error of at most 0.0003.
Values sent between devices are 32-bit elements; how exact they have to be, the bound alone decides.
No kernel may reach another device: no remote copies, remote signals or barrier semaphores. Data moves between devices by JAX's collectives and lax.ppermute only.
A program may use at most 192 MiB of HBM per device.

```python
import jax
import jax.numpy as jnp
from jax import lax

FEAT = 9
CENTRES = 16384
POINTS = 65536


def upper_factor(key, noise):
    diagonal = jnp.exp(jax.random.uniform(key, (CENTRES, 1), jnp.float32, 0.0, 0.6931472))
    row_ids = lax.broadcasted_iota(jnp.int32, (CENTRES, CENTRES), 0)
    col_ids = lax.broadcasted_iota(jnp.int32, (CENTRES, CENTRES), 1)
    above = noise * (0.7 / CENTRES ** 0.5)
    on_diag = jnp.broadcast_to(diagonal, (CENTRES, CENTRES))
    return jnp.where(col_ids > row_ids, above, jnp.where(col_ids == row_ids, on_diag, 0.0)).astype(jnp.float32)


def draw_t_inverse(key, part):
    key = jax.random.fold_in(key, 11)
    first_key, second_key = jax.random.split(key)
    noise = jax.random.normal(second_key, (CENTRES, CENTRES), jnp.float32)
    return upper_factor(first_key, noise)


def draw_a_inverse(key, part):
    key = jax.random.fold_in(key, 12)
    first_key, second_key = jax.random.split(key)
    noise = jax.random.normal(second_key, (CENTRES, CENTRES), jnp.float32)
    return upper_factor(first_key, noise)


def level_of(key, shape, shards, low, largest):
    def one(axis_at, shards_of):
        steps = jax.random.uniform(jax.random.fold_in(jax.random.fold_in(key, 6), axis_at), (shards_of,), jnp.float32, low / len(shards), largest / len(shards))
        return jnp.repeat(jnp.exp(steps), shape[axis_at] // shards_of).reshape((-1,) + (1,) * (len(shape) - axis_at - 1))

    level = one(*shards[0])
    for cut in shards[1:]:
        level = level * one(*cut)
    return level


def gaussian(rng, shape, width, reach, cuts=(), kind=jnp.bfloat16):
    entries = width * jax.random.normal(rng, shape, jnp.float32)
    if cuts:
        entries = entries * level_of(rng, shape, cuts, -0.22, 0.18)
    return jnp.clip(entries, -reach, reach).astype(kind)


def setup_inputs(seed: int = 0) -> dict:
    keys = jax.random.split(jax.random.key(seed), 8)
    return {
        "points": gaussian(keys[0], (FEAT, POINTS), 2.0, 6.0, ((1, 8),), jnp.float32),
        "centres": gaussian(keys[1], (FEAT, CENTRES), 2.0, 6.0, ((1, 4),), jnp.float32),
        "t_inverse": draw_t_inverse(jax.random.fold_in(keys[7], 71), 0),
        "a_inverse": draw_a_inverse(jax.random.fold_in(keys[7], 71), 0),
        "solution": gaussian(keys[4], (CENTRES,), 1.0, 6.0, ((0, 4),), jnp.float32),
        "residual": gaussian(keys[5], (CENTRES,), 1.0, 6.0, ((0, 4),), jnp.float32),
        "direction": gaussian(keys[6], (CENTRES,), 1.0, 6.0, ((0, 4),), jnp.float32),
    }


ridge_weight = 0.1


def kernel_block(point_block, centres, centre_norms):
    cross = lax.dot_general(point_block, centres, (((0,), (0,)), ((), ())), precision=lax.Precision.HIGHEST)
    point_norms = jnp.sum(point_block * point_block, axis=0)
    distance = point_norms[:, None] + centre_norms[None, :] - 2.0 * cross
    return jnp.exp(-distance / FEAT)


def reference(points, centres, t_inverse, a_inverse, solution, residual, direction):
    highest = lax.Precision.HIGHEST
    first_solve = jnp.dot(a_inverse, direction, precision=highest)
    weights = jnp.dot(t_inverse, first_solve, precision=highest)
    centre_norms = jnp.sum(centres * centres, axis=0)
    block = min(1024, POINTS)
    count = POINTS // block

    def step(running, position):
        point_block = lax.dynamic_slice_in_dim(points, (position * block).astype(jnp.int32), block, 1)
        tile = kernel_block(point_block, centres, centre_norms)
        fitted = jnp.dot(tile, weights, precision=highest)
        return running + jnp.dot(fitted, tile, precision=highest), None

    back, _ = lax.scan(step, jnp.zeros((CENTRES,), jnp.float32), jnp.arange(count, dtype=jnp.int32))
    back = back / POINTS
    inner = jnp.dot(back, t_inverse, precision=highest) + ridge_weight * first_solve
    image = jnp.dot(inner, a_inverse, precision=highest)
    norm_old = jnp.sum(residual * residual)
    alpha = norm_old / jnp.sum(direction * image)
    new_solution = solution + alpha * direction
    new_residual = residual - alpha * image
    norm_new = jnp.sum(new_residual * new_residual)
    new_direction = new_residual + (norm_new / norm_old) * direction
    return new_solution, new_residual, new_direction
```

```python
import functools

import jax
import jax.numpy as jnp
from jax import lax
from jax.experimental import pallas as pl
from jax.experimental.pallas import tpu as pltpu
from jax.sharding import PartitionSpec as P

ridge_weight = 0.1
log2_e = 1.4426950408889634
LANES = 128
GROUP = 16
GROUPS = 6
PART = 256
MIB = 1024 * 1024
BOTH = ("dp", "centre")


def params(mib):
    return pltpu.CompilerParams(vmem_limit_bytes=mib * MIB)


def whole(shape):
    return pl.BlockSpec(shape, lambda *_: (0,) * len(shape))


def row_product(tile_ref, vec_ref):
    total = None
    for k in range(vec_ref.shape[0]):
        term = tile_ref[:, k * LANES:(k + 1) * LANES] * vec_ref[k:k + 1, :]
        total = term if total is None else total + term
    return jnp.sum(total.T, axis=0, keepdims=True)


def write_all(out_ref, rows_ref):
    for place in range(out_ref.shape[0]):
        out_ref[place] = rows_ref[...]


def start_stream(matrix_ref, held_ref, sems):
    copies = []
    for i in range(matrix_ref.shape[0] // LANES):
        rows = pl.ds(i * LANES, LANES)
        copies.append(pltpu.make_async_copy(matrix_ref.at[rows, :], held_ref.at[rows, :], sems.at[i]))
        copies[-1].start()
    return copies


def stream_rows(copies, held_ref, vec_ref, rows_ref, out_ref):
    for i, copy in enumerate(copies):
        copy.wait()
        rows_ref[i:i + 1, :] = row_product(held_ref.at[i * LANES:(i + 1) * LANES, :], vec_ref)
    write_all(out_ref, rows_ref)


def forward_direction(matrix_ref, vec_ref, out_ref, rows_ref, held_ref, sems):
    stream_rows(start_stream(matrix_ref, held_ref, sems), held_ref, vec_ref, rows_ref, out_ref)


def forward_gathered(centre_size, matrix_ref, gathered_ref, out_ref, rows_ref, vec_ref, held_ref, sems):
    copies = start_stream(matrix_ref, held_ref, sems)
    deep = rows_ref.shape[0]
    blocks = vec_ref.shape[0] // deep
    first = lax.axis_index("centre") * blocks
    for i in range(blocks):
        part = gathered_ref[pl.ds((first + i) * centre_size, centre_size)]
        vec_ref[i * deep:(i + 1) * deep, :] = jnp.sum(part, axis=0)
    stream_rows(copies, held_ref, vec_ref, rows_ref, out_ref)


def column_of(row):
    return jnp.broadcast_to(row, (LANES, LANES)).T


def column_sums(copies, held_ref, vec_ref, sums_ref, whole_ref):
    sums_ref[...] = jnp.zeros_like(sums_ref)
    for i, copy in enumerate(copies):
        spread = column_of(vec_ref[i:i + 1, :])
        copy.wait()
        for k in range(held_ref.shape[1] // LANES):
            product = held_ref[i * LANES:(i + 1) * LANES, k * LANES:(k + 1) * LANES] * spread
            sums_ref[:, k * LANES:(k + 1) * LANES] += jnp.sum(product.reshape(LANES // 8, 8, LANES), axis=0)
    for k in range(whole_ref.shape[0]):
        whole_ref[k:k + 1, :] = jnp.sum(sums_ref[:, k * LANES:(k + 1) * LANES], axis=0, keepdims=True)


def back_t(scale, matrix_ref, gathered_ref, out_ref, vec_ref, sums_ref, whole_ref, held_ref, sems):
    copies = start_stream(matrix_ref, held_ref, sems)
    vec_ref[...] = jnp.sum(gathered_ref[...], axis=0) * scale
    column_sums(copies, held_ref, vec_ref, sums_ref, whole_ref)
    deep = vec_ref.shape[0]
    blocks = whole_ref.shape[0] // deep
    per = out_ref.shape[0] // lax.axis_size("dp")
    for place in range(out_ref.shape[0]):
        half = (place // per) % blocks
        out_ref[place] = whole_ref[half * deep:(half + 1) * deep, :]


def back_a(matrix_ref, gathered_ref, solved_ref, out_ref, vec_ref, sums_ref, whole_ref, held_ref, sems):
    copies = start_stream(matrix_ref, held_ref, sems)
    deep = vec_ref.shape[0]
    dp_size = lax.axis_size("dp")
    centre_size = lax.axis_size("centre")
    blocks = whole_ref.shape[0] // deep
    place = lax.axis_index("dp")
    source = place // blocks
    solved = jnp.sum(solved_ref[pl.ds(place * centre_size, centre_size)], axis=0)
    total = gathered_ref[source]
    for p in range(1, dp_size):
        total = total + gathered_ref[p * centre_size + source]
    inner = total + ridge_weight * solved
    vec_ref[...] = inner
    dot = jnp.full((8, LANES), jnp.sum(inner * solved), jnp.float32)
    column_sums(copies, held_ref, vec_ref, sums_ref, whole_ref)
    size = whole_ref.shape[0]
    for place in range(out_ref.shape[0]):
        out_ref[place, :size, :] = whole_ref[...]
        out_ref[place, size:, :] = dot


def rounded(values):
    return values.astype(jnp.bfloat16).astype(jnp.float32)


def three(values):
    first = rounded(values)
    rest = values - first
    second = rounded(rest)
    return first, second, rounded(rest - second)


def store_group(target_ref, group, start, features, norm, ones, norm_first):
    width = features.shape[1]
    rows = (norm, ones) if norm_first else (ones, norm)
    pad = jnp.zeros((GROUP - features.shape[0] - 2, width), jnp.float32)
    block = jnp.concatenate([features, rows[0], rows[1], pad], axis=0)
    target_ref[group * GROUP:(group + 1) * GROUP, pl.ds(start, width)] = block.astype(target_ref.dtype)


def store_splits(target_ref, start, values, norms, order, norm_first):
    pieces = three(values)
    norm_pieces = three(norms)
    one = jnp.ones_like(norms)
    zero = jnp.zeros_like(norms)
    for group in range(GROUPS):
        has = group < 3
        store_group(
            target_ref, group, start, pieces[order[group]],
            norm_pieces[group] if has else zero, one if has else zero, norm_first,
        )


def operands(feat, points_ref, own_ref, one_ref, two_ref, three_ref, after_ref, x_ref, c_ref, rr_ref, rows_x):
    del after_ref
    centre_size = lax.axis_size("centre")
    here = lax.axis_index("centre")
    mine = x_ref.shape[0]
    share = c_ref.shape[1] // centre_size
    part = own_ref.shape[1] - share
    scale = log2_e / feat
    x = points_ref[:, pl.ds(pl.multiple_of(here * mine, LANES), mine)]
    norms = -scale * jnp.sum(x * x, axis=0, keepdims=True)
    store_splits(rows_x, 0, x, norms, (0, 0, 1, 1, 0, 2), True)
    for r in range(mine // LANES):
        x_ref[r * LANES:(r + 1) * LANES, :] = rows_x[:, r * LANES:(r + 1) * LANES].T.astype(jnp.bfloat16)
    rr = jnp.zeros((1, 1), jnp.float32)
    for back_by, piece in enumerate((own_ref, one_ref, two_ref, three_ref)):
        place = lax.rem(here + centre_size - back_by, centre_size)
        start = pl.multiple_of(place * share, LANES)
        for s in range(share // part):
            c = jnp.concatenate([piece[:, s * part:(s + 1) * part], piece[s:s + 1, share:]], axis=0)
            norms = -scale * jnp.sum(c * c, axis=0, keepdims=True)
            at = pl.multiple_of(start + s * part, LANES)
            store_splits(c_ref, at, c * (2.0 * scale), norms, (0, 1, 0, 1, 2, 0), False)
            res = piece[4 + s:5 + s, share:]
            rr = rr + jnp.sum(res * res, axis=1, keepdims=True)
    rr_ref[...] = jnp.broadcast_to(rr, rr_ref.shape)


def kernel_products(block, chunk, x_ref, c_ref, gathered_ref, out_ref, w_ref, tile_ref, fit_ref, f_ref, back_ref):
    centre_size = lax.axis_size("centre")
    dp_size = lax.axis_size("dp")
    deep = gathered_ref.shape[1]
    width = chunk // LANES
    chunks = c_ref.shape[1] // chunk
    for p in range(dp_size):
        w_ref[p * deep:(p + 1) * deep, :] = jnp.sum(gathered_ref[p * centre_size:(p + 1) * centre_size], axis=0)
    back_ref[...] = jnp.zeros_like(back_ref)
    f_ref[...] = jnp.zeros_like(f_ref)

    def points_block(step, carry):
        fit_ref[...] = jnp.zeros_like(fit_ref)

        def first_pass(n, carry):
            at = pl.multiple_of(n * chunk, chunk)
            c = c_ref[:, pl.ds(at, chunk)]
            for r in range(0, block, PART):
                x = x_ref[pl.ds(pl.multiple_of(step * block + r, PART), PART), :]
                power = jnp.dot(x, c, preferred_element_type=jnp.float32)
                value = jnp.exp2(power)
                tile_ref[r:r + PART, pl.ds(at, chunk)] = value.astype(jnp.bfloat16)
                total = fit_ref[r:r + PART, :]
                for k in range(width):
                    total = total + value[:, k * LANES:(k + 1) * LANES] * w_ref[pl.ds(n * width + k, 1), :]
                fit_ref[r:r + PART, :] = total
            return carry

        lax.fori_loop(0, chunks, first_pass, 0, unroll=16)
        for r in range(0, block, LANES):
            f = jnp.sum(fit_ref[r:r + LANES, :].T, axis=0, keepdims=True)
            first = rounded(f)
            rows = jnp.concatenate([first, f - first, jnp.zeros((14, LANES), jnp.float32)], axis=0)
            f_ref[:, r:r + LANES] = rows.astype(jnp.bfloat16)

        def second_pass(n, carry):
            at = pl.multiple_of(n * 512, 512)
            back_ref[:, pl.ds(at, 512)] += jnp.dot(
                f_ref[...], tile_ref[:, pl.ds(at, 512)], preferred_element_type=jnp.float32
            )
            return carry

        lax.fori_loop(0, c_ref.shape[1] // 512, second_pass, 0, unroll=16)
        return carry

    lax.fori_loop(0, x_ref.shape[0] // block, points_block, 0)
    for p in range(dp_size):
        for k in range(deep):
            at = (p * deep + k) * LANES
            row = back_ref[0:1, at:at + LANES] + back_ref[1:2, at:at + LANES]
            for c in range(centre_size):
                out_ref[p * centre_size + c, k:k + 1, :] = row


def update(gathered_ref, rr_ref, solution_ref, residual_ref, direction_ref, new_solution_ref, new_residual_ref, norm_ref):
    size = solution_ref.shape[0]
    total = jnp.sum(gathered_ref[...], axis=0)
    alpha = rr_ref[0:1, 0:1] / total[size:size + 1, 0:1]
    new_solution_ref[...] = solution_ref[...] + alpha * direction_ref[...]
    new_residual = residual_ref[...] - alpha * total[:size]
    new_residual_ref[...] = new_residual
    norm_ref[...] = jnp.full(norm_ref.shape, jnp.sum(new_residual * new_residual), jnp.float32)


def finish(norms_ref, rr_ref, new_residual_ref, direction_ref, out_ref):
    norm_new = jnp.sum(norms_ref[...], axis=0)[0:1, 0:1]
    out_ref[...] = new_residual_ref[...] + (norm_new / rr_ref[0:1, 0:1]) * direction_ref[...]


def body(points, centres, t_inverse, a_inverse, solution, residual, direction):
    f32 = jnp.float32
    rows_block, cols_block = t_inverse.shape
    feat = points.shape[0]
    dp_size = lax.axis_size("dp")
    centre_size = lax.axis_size("centre")
    devices = dp_size * centre_size
    deep = rows_block // LANES
    wide = cols_block // LANES
    count = points.shape[1] * dp_size
    mine = points.shape[1] // centre_size
    total = cols_block * centre_size
    shape = jax.ShapeDtypeStruct
    spread_shape = (devices, deep, LANES)
    sums = pltpu.VMEM((8, cols_block), f32)

    in_vmem = pl.BlockSpec(memory_space=pltpu.VMEM)
    anywhere = pl.BlockSpec(memory_space=pl.ANY)
    matrix_bytes = rows_block * cols_block * 4
    matrix_cost = pl.CostEstimate(flops=2 * rows_block * cols_block, bytes_accessed=matrix_bytes, transcendentals=0)

    def exchange(values, axes):
        return lax.all_to_all(values, axes, 0, 0, tiled=True)

    stream = [pltpu.VMEM((rows_block, cols_block), f32), pltpu.SemaphoreType.DMA((deep,))]
    rows = pltpu.VMEM((deep, LANES), f32)
    cols = pltpu.VMEM((wide, LANES), f32)
    a_source = pltpu.with_memory_space_constraint(a_inverse, pltpu.HBM)
    t_source = pltpu.with_memory_space_constraint(t_inverse, pltpu.HBM)

    part = cols_block // 4
    tail = jnp.concatenate([centres[8].reshape(4, part), residual.reshape(4, part)], axis=0)
    own = jnp.concatenate([centres[:8], tail], axis=1)
    moved = [
        lax.ppermute(own, "centre", [(i, (i + by) % centre_size) for i in range(centre_size)])
        for by in range(1, centre_size)
    ]
    direction_rows = direction.reshape(wide, LANES)
    first = pl.pallas_call(
        forward_direction, out_shape=shape(spread_shape, f32),
        in_specs=[anywhere, in_vmem], out_specs=in_vmem,
        scratch_shapes=[rows] + stream,
        cost_estimate=matrix_cost, compiler_params=params(36), name="solve_a",
    )(a_source, direction_rows)
    first, moved = lax.optimization_barrier((first, moved))
    solved = exchange(first, BOTH)
    second = pl.pallas_call(
        functools.partial(forward_gathered, centre_size), out_shape=shape(spread_shape, f32),
        in_specs=[anywhere, in_vmem], out_specs=in_vmem, scratch_shapes=[rows, cols] + stream,
        cost_estimate=matrix_cost, compiler_params=params(36), name="solve_t",
    )(t_source, solved)
    weights = exchange(second, BOTH)
    block, chunk = 512, 256
    depth = GROUP * GROUPS
    x_rows, c_rows, rr = pl.pallas_call(
        functools.partial(operands, feat),
        out_shape=(shape((mine, depth), jnp.bfloat16), shape((depth, total), jnp.bfloat16), shape((8, LANES), f32)),
        in_specs=[in_vmem] * 5 + [anywhere], out_specs=(in_vmem,) * 3,
        scratch_shapes=[pltpu.VMEM((depth, mine), f32)],
        compiler_params=params(12), name="operands",
    )(points, own, *moved, second)
    back = pl.pallas_call(
        functools.partial(kernel_products, block, chunk), out_shape=shape(spread_shape, f32),
        in_specs=[in_vmem] * 3, out_specs=in_vmem,
        scratch_shapes=[
            pltpu.VMEM((total // LANES, LANES), f32),
            pltpu.VMEM((block, total), jnp.bfloat16),
            pltpu.VMEM((block, LANES), f32),
            pltpu.VMEM((16, block), jnp.bfloat16),
            pltpu.VMEM((16, total), f32),
        ],
        compiler_params=params(24), name="kernel_pair",
    )(x_rows, c_rows, weights)
    back_all = exchange(back, BOTH)
    third = pl.pallas_call(
        functools.partial(back_t, 1.0 / count), out_shape=shape(spread_shape, f32),
        in_specs=[anywhere, in_vmem], out_specs=in_vmem, scratch_shapes=[rows, sums, cols] + stream,
        cost_estimate=matrix_cost, compiler_params=params(36), name="back_t",
    )(t_source, back_all)
    inner_all = exchange(third, BOTH)
    image_shape = (dp_size, wide + 8, LANES)
    fourth = pl.pallas_call(
        back_a, out_shape=shape(image_shape, f32),
        in_specs=[anywhere, in_vmem, in_vmem], out_specs=in_vmem, scratch_shapes=[rows, sums, cols] + stream,
        cost_estimate=matrix_cost, compiler_params=params(36), name="back_a",
    )(a_source, inner_all, solved)
    image_all = exchange(fourth, "dp")
    vec = shape((wide, LANES), f32)
    new_solution, new_residual, norm = pl.pallas_call(
        update, out_shape=(vec, vec, shape((centre_size, 8, LANES), f32)), compiler_params=params(8), name="update",
    )(image_all, rr, solution.reshape(wide, LANES), residual.reshape(wide, LANES), direction_rows)
    norms = exchange(norm, "centre")
    new_direction = pl.pallas_call(
        finish, out_shape=vec, compiler_params=params(8), name="finish",
    )(norms, rr, new_residual, direction_rows)
    return new_solution.reshape(-1), new_residual.reshape(-1), new_direction.reshape(-1)


def solution(mesh):
    placed = (
        P(None, "dp"),
        P(None, "centre"),
        P("dp", "centre"),
        P("dp", "centre"),
        P("centre"),
        P("centre"),
        P("centre"),
    )
    return jax.shard_map(
        body,
        mesh=mesh,
        in_specs=placed,
        out_specs=(P("centre"), P("centre"), P("centre")),
        check_vma=False,
    )
```

```python
import functools

import jax
import jax.numpy as jnp
from jax import lax
from jax.experimental import pallas as pl
from jax.experimental.pallas import tpu as pltpu
from jax.sharding import PartitionSpec as P

ridge_weight = 0.1
log2_e = 1.4426950408889634
LANES = 128
DEPTH = 64
PART = 256
PAIR = 1024
MIB = 1024 * 1024
BOTH = ("dp", "centre")


def params(mib):
    return pltpu.CompilerParams(vmem_limit_bytes=mib * MIB)


def whole(shape):
    return pl.BlockSpec(shape, lambda *_: (0,) * len(shape))


def row_product(tile_ref, vec_ref):
    total = None
    for k in range(vec_ref.shape[0]):
        term = tile_ref[:, k * LANES:(k + 1) * LANES] * vec_ref[k:k + 1, :]
        total = term if total is None else total + term
    return jnp.sum(total.T, axis=0, keepdims=True)


def write_all(out_ref, rows_ref):
    for place in range(out_ref.shape[0]):
        out_ref[place] = rows_ref[...]


def start_stream(matrix_ref, held_ref, sems):
    copies = []
    for i in range(matrix_ref.shape[0] // LANES):
        rows = pl.ds(i * LANES, LANES)
        copies.append(pltpu.make_async_copy(matrix_ref.at[rows, :], held_ref.at[rows, :], sems.at[i]))
        copies[-1].start()
    return copies


def stream_rows(copies, held_ref, vec_ref, rows_ref, out_ref):
    for i, copy in enumerate(copies):
        copy.wait()
        rows_ref[i:i + 1, :] = row_product(held_ref.at[i * LANES:(i + 1) * LANES, :], vec_ref)
    write_all(out_ref, rows_ref)


def forward_direction(matrix_ref, vec_ref, out_ref, rows_ref, held_ref, sems):
    stream_rows(start_stream(matrix_ref, held_ref, sems), held_ref, vec_ref, rows_ref, out_ref)


def forward_gathered(centre_size, matrix_ref, gathered_ref, out_ref, rows_ref, vec_ref, held_ref, sems):
    copies = start_stream(matrix_ref, held_ref, sems)
    deep = rows_ref.shape[0]
    blocks = vec_ref.shape[0] // deep
    first = lax.axis_index("centre") * blocks
    for i in range(blocks):
        part = gathered_ref[pl.ds((first + i) * centre_size, centre_size)]
        vec_ref[i * deep:(i + 1) * deep, :] = jnp.sum(part, axis=0)
    stream_rows(copies, held_ref, vec_ref, rows_ref, out_ref)


def column_of(row):
    return jnp.broadcast_to(row, (LANES, LANES)).T


def column_sums(copies, held_ref, vec_ref, sums_ref, whole_ref):
    sums_ref[...] = jnp.zeros_like(sums_ref)
    for i, copy in enumerate(copies):
        spread = column_of(vec_ref[i:i + 1, :])
        copy.wait()
        for k in range(held_ref.shape[1] // LANES):
            product = held_ref[i * LANES:(i + 1) * LANES, k * LANES:(k + 1) * LANES] * spread
            sums_ref[:, k * LANES:(k + 1) * LANES] += jnp.sum(product.reshape(LANES // 8, 8, LANES), axis=0)
    for k in range(whole_ref.shape[0]):
        whole_ref[k:k + 1, :] = jnp.sum(sums_ref[:, k * LANES:(k + 1) * LANES], axis=0, keepdims=True)


def back_t(scale, matrix_ref, gathered_ref, out_ref, vec_ref, sums_ref, whole_ref, held_ref, sems):
    copies = start_stream(matrix_ref, held_ref, sems)
    vec_ref[...] = jnp.sum(gathered_ref[...], axis=0) * scale
    column_sums(copies, held_ref, vec_ref, sums_ref, whole_ref)
    deep = vec_ref.shape[0]
    blocks = whole_ref.shape[0] // deep
    per = out_ref.shape[0] // lax.axis_size("dp")
    for place in range(out_ref.shape[0]):
        half = (place // per) % blocks
        out_ref[place] = whole_ref[half * deep:(half + 1) * deep, :]


def back_a(matrix_ref, gathered_ref, solved_ref, out_ref, vec_ref, sums_ref, whole_ref, held_ref, sems):
    copies = start_stream(matrix_ref, held_ref, sems)
    deep = vec_ref.shape[0]
    dp_size = lax.axis_size("dp")
    centre_size = lax.axis_size("centre")
    blocks = whole_ref.shape[0] // deep
    place = lax.axis_index("dp")
    source = place // blocks
    solved = jnp.sum(solved_ref[pl.ds(place * centre_size, centre_size)], axis=0)
    total = gathered_ref[source]
    for p in range(1, dp_size):
        total = total + gathered_ref[p * centre_size + source]
    inner = total + ridge_weight * solved
    vec_ref[...] = inner
    dot = jnp.full((8, LANES), jnp.sum(inner * solved), jnp.float32)
    column_sums(copies, held_ref, vec_ref, sums_ref, whole_ref)
    size = whole_ref.shape[0]
    for place in range(out_ref.shape[0]):
        out_ref[place, :size, :] = whole_ref[...]
        out_ref[place, size:, :] = dot


def rounded(values):
    return values.astype(jnp.bfloat16).astype(jnp.float32)


def three(values):
    first = rounded(values)
    rest = values - first
    second = rounded(rest)
    return first, second, rounded(rest - second)


def store_splits(target_ref, start, values, norms, order, norm_first):
    width = values.shape[1]
    pieces = three(values)
    norm_rows = list(three(norms))
    ones = [jnp.ones_like(norms)] * 3
    last = [pieces[i][8:9] for i in order] + (norm_rows + ones if norm_first else ones + norm_rows)
    tail = jnp.concatenate(last + [jnp.zeros((4, width), jnp.float32)], axis=0)
    groups = [pieces[i][:8] for i in order] + [tail[:8], tail[8:]]
    for row in range(0, len(groups), 2):
        pair = jnp.concatenate(groups[row:row + 2], axis=0)
        target_ref[row * 8:row * 8 + 16, pl.ds(start, width)] = pair.astype(target_ref.dtype)


def half_start(width, other):
    return pl.multiple_of(lax.rem(lax.axis_index("dp") + other, 2) * width, LANES)


def pack(centres_ref, residual_ref, after_ref, own_ref, half_ref):
    del after_ref
    share = centres_ref.shape[1]
    part = share // 4
    own_ref[:, :share] = centres_ref[:8, :]
    for s in range(4):
        own_ref[s:s + 1, share:] = centres_ref[8:9, s * part:(s + 1) * part]
        own_ref[4 + s:5 + s, share:] = residual_ref[:, s * part:(s + 1) * part]
    width = half_ref.shape[1]
    half_ref[...] = own_ref[:, pl.ds(half_start(width, 0), width)]


def operands(feat, steps, points_ref, own_ref, *refs):
    halves, (after_ref, x_ref, c_ref, rr_ref, rows_x, points_v, pieces, sems) = refs[:2 * steps], refs[2 * steps:]
    del after_ref
    centre_size = lax.axis_size("centre")
    here = lax.axis_index("centre")
    mine = x_ref.shape[0]
    share = c_ref.shape[1] // centre_size
    part = share // 4
    width = halves[0].shape[1]
    start = pl.multiple_of(here * mine, LANES)
    copies = [
        pltpu.make_async_copy(points_ref.at[:, pl.ds(start, mine)], points_v, sems.at[0]),
        pltpu.make_async_copy(own_ref, pieces.at[0], sems.at[1]),
    ]
    for i, half in enumerate(halves):
        place = pieces.at[1 + i % steps, :, pl.ds(half_start(width, i // steps), width)]
        copies.append(pltpu.make_async_copy(half, place, sems.at[2 + i]))
    for copy in copies:
        copy.start()
    for copy in copies:
        copy.wait()
    scale = log2_e / feat
    x = points_v[...]
    norms = -scale * jnp.sum(x * x, axis=0, keepdims=True)
    store_splits(rows_x, 0, x, norms, (0, 0, 1, 1, 0, 2), True)
    for r in range(mine // LANES):
        x_ref[r * LANES:(r + 1) * LANES, :] = rows_x[:, r * LANES:(r + 1) * LANES].T.astype(jnp.bfloat16)
    rr = jnp.zeros((1, 1), jnp.float32)
    for back_by in range(steps + 1):
        place = lax.rem(here + centre_size - back_by, centre_size)
        start = pl.multiple_of(place * share, LANES)
        for s in range(4):
            c = jnp.concatenate([pieces[back_by, :, s * part:(s + 1) * part], pieces[back_by, s:s + 1, share:]], axis=0)
            norms = -scale * jnp.sum(c * c, axis=0, keepdims=True)
            at = pl.multiple_of(start + s * part, LANES)
            store_splits(c_ref, at, c * (2.0 * scale), norms, (0, 1, 0, 1, 2, 0), False)
            res = pieces[back_by, 4 + s:5 + s, share:]
            rr = rr + jnp.sum(res * res, axis=1, keepdims=True)
    rr_ref[...] = jnp.broadcast_to(rr, rr_ref.shape)


def kernel_products(block, chunk, x_ref, c_ref, gathered_ref, out_ref, w_ref, tile_ref, fit_ref, f_ref, back_ref):
    centre_size = lax.axis_size("centre")
    dp_size = lax.axis_size("dp")
    deep = gathered_ref.shape[1]
    width = chunk // LANES
    chunks = c_ref.shape[1] // chunk
    for p in range(dp_size):
        w_ref[p * deep:(p + 1) * deep, :] = jnp.sum(gathered_ref[p * centre_size:(p + 1) * centre_size], axis=0)
    back_ref[...] = jnp.zeros_like(back_ref)
    f_ref[...] = jnp.zeros_like(f_ref)

    def points_block(step, carry):
        fit_ref[...] = jnp.zeros_like(fit_ref)

        def first_pass(n, carry):
            at = pl.multiple_of(n * chunk, chunk)
            c = c_ref[:, pl.ds(at, chunk)]
            for r in range(0, block, PART):
                x = x_ref[pl.ds(pl.multiple_of(step * block + r, PART), PART), :]
                power = jnp.dot(x, c, preferred_element_type=jnp.float32)
                value = jnp.exp2(power)
                tile_ref[r:r + PART, pl.ds(at, chunk)] = value.astype(jnp.bfloat16)
                total = fit_ref[r:r + PART, :]
                for k in range(width):
                    total = total + value[:, k * LANES:(k + 1) * LANES] * w_ref[pl.ds(n * width + k, 1), :]
                fit_ref[r:r + PART, :] = total
            return carry

        lax.fori_loop(0, chunks, first_pass, 0, unroll=16)
        for r in range(0, block, LANES):
            f = jnp.sum(fit_ref[r:r + LANES, :].T, axis=0, keepdims=True)
            first = rounded(f)
            rows = jnp.concatenate([first, f - first, jnp.zeros((14, LANES), jnp.float32)], axis=0)
            f_ref[:, r:r + LANES] = rows.astype(jnp.bfloat16)

        def second_pass(n, carry):
            at = pl.multiple_of(n * PAIR, PAIR)
            back_ref[:, pl.ds(at, PAIR)] += jnp.dot(
                f_ref[...], tile_ref[:, pl.ds(at, PAIR)], preferred_element_type=jnp.float32
            )
            return carry

        lax.fori_loop(0, c_ref.shape[1] // PAIR, second_pass, 0, unroll=16)
        return carry

    lax.fori_loop(0, x_ref.shape[0] // block, points_block, 0)
    for p in range(dp_size):
        for k in range(deep):
            at = (p * deep + k) * LANES
            row = back_ref[0:1, at:at + LANES] + back_ref[1:2, at:at + LANES]
            for c in range(centre_size):
                out_ref[p * centre_size + c, k:k + 1, :] = row


def update(gathered_ref, rr_ref, solution_ref, residual_ref, direction_ref, new_solution_ref, new_residual_ref, norm_ref):
    size = solution_ref.shape[0]
    total = jnp.sum(gathered_ref[...], axis=0)
    alpha = rr_ref[0:1, 0:1] / total[size:size + 1, 0:1]
    new_solution_ref[...] = solution_ref[...] + alpha * direction_ref[...]
    new_residual = residual_ref[...] - alpha * total[:size]
    new_residual_ref[...] = new_residual
    norm_ref[...] = jnp.full(norm_ref.shape, jnp.sum(new_residual * new_residual), jnp.float32)


def finish(norms_ref, rr_ref, new_residual_ref, direction_ref, out_ref):
    norm_new = jnp.sum(norms_ref[...], axis=0)[0:1, 0:1]
    out_ref[...] = new_residual_ref[...] + (norm_new / rr_ref[0:1, 0:1]) * direction_ref[...]


def body(points, centres, t_inverse, a_inverse, solution, residual, direction):
    f32 = jnp.float32
    rows_block, cols_block = t_inverse.shape
    feat = points.shape[0]
    dp_size = lax.axis_size("dp")
    centre_size = lax.axis_size("centre")
    devices = dp_size * centre_size
    deep = rows_block // LANES
    wide = cols_block // LANES
    count = points.shape[1] * dp_size
    mine = points.shape[1] // centre_size
    total = cols_block * centre_size
    shape = jax.ShapeDtypeStruct
    spread_shape = (devices, deep, LANES)
    sums = pltpu.VMEM((8, cols_block), f32)

    in_vmem = pl.BlockSpec(memory_space=pltpu.VMEM)
    anywhere = pl.BlockSpec(memory_space=pl.ANY)
    matrix_bytes = rows_block * cols_block * 4
    matrix_cost = pl.CostEstimate(flops=2 * rows_block * cols_block, bytes_accessed=matrix_bytes, transcendentals=0)

    def exchange(values, axes):
        return lax.all_to_all(values, axes, 0, 0, tiled=True)

    stream = [pltpu.VMEM((rows_block, cols_block), f32), pltpu.SemaphoreType.DMA((deep,))]
    rows = pltpu.VMEM((deep, LANES), f32)
    cols = pltpu.VMEM((wide, LANES), f32)
    a_source = pltpu.with_memory_space_constraint(a_inverse, pltpu.HBM)
    t_source = pltpu.with_memory_space_constraint(t_inverse, pltpu.HBM)

    direction_rows = direction.reshape(wide, LANES)
    first = pl.pallas_call(
        forward_direction, out_shape=shape(spread_shape, f32),
        in_specs=[anywhere, in_vmem], out_specs=in_vmem,
        scratch_shapes=[rows] + stream,
        cost_estimate=matrix_cost, compiler_params=params(36), name="solve_a",
    )(a_source, direction_rows)
    packed = cols_block + cols_block // 4
    own, half = pl.pallas_call(
        pack, out_shape=(shape((8, packed), f32), shape((8, packed // 2), f32)), in_specs=[in_vmem, in_vmem, anywhere],
        out_specs=(in_vmem,) * 2, compiler_params=params(4), name="pack",
    )(centres, residual.reshape(1, cols_block), first)
    steps = centre_size - 1
    moved = [
        lax.ppermute(half, "centre", [(i, (i + by) % centre_size) for i in range(centre_size)])
        for by in range(1, centre_size)
    ]
    solved = exchange(first, BOTH)
    second = pl.pallas_call(
        functools.partial(forward_gathered, centre_size), out_shape=shape(spread_shape, f32),
        in_specs=[anywhere, in_vmem], out_specs=in_vmem, scratch_shapes=[rows, cols] + stream,
        cost_estimate=matrix_cost, compiler_params=params(36), name="solve_t",
    )(t_source, solved)
    second, moved = lax.optimization_barrier((second, moved))
    weights = exchange(second, BOTH)
    swapped = [lax.ppermute(piece, "dp", [(i, i ^ 1) for i in range(dp_size)]) for piece in moved]
    block, chunk = min(1024, mine), 256
    sources = [pltpu.with_memory_space_constraint(v, pltpu.HBM) for v in [points, own] + list(moved) + swapped]
    x_rows, c_rows, rr = pl.pallas_call(
        functools.partial(operands, feat, steps),
        out_shape=(shape((mine, DEPTH), jnp.bfloat16), shape((DEPTH, total), jnp.bfloat16), shape((8, LANES), f32)),
        in_specs=[anywhere] * (3 + 2 * steps), out_specs=(in_vmem,) * 3,
        scratch_shapes=[
            pltpu.VMEM((DEPTH, mine), f32), pltpu.VMEM((feat, mine), f32), pltpu.VMEM((steps + 1, 8, packed), f32),
            pltpu.SemaphoreType.DMA((2 + 2 * steps,)),
        ],
        compiler_params=params(12), name="operands",
    )(*sources, second)
    back = pl.pallas_call(
        functools.partial(kernel_products, block, chunk), out_shape=shape(spread_shape, f32),
        in_specs=[in_vmem] * 3, out_specs=in_vmem,
        scratch_shapes=[
            pltpu.VMEM((total // LANES, LANES), f32),
            pltpu.VMEM((block, total), jnp.bfloat16),
            pltpu.VMEM((block, LANES), f32),
            pltpu.VMEM((16, block), jnp.bfloat16),
            pltpu.VMEM((16, total), f32),
        ],
        compiler_params=params(42), name="kernel_pair",
    )(x_rows, c_rows, weights)
    back_all = exchange(back, BOTH)
    third = pl.pallas_call(
        functools.partial(back_t, 1.0 / count), out_shape=shape(spread_shape, f32),
        in_specs=[anywhere, in_vmem], out_specs=in_vmem, scratch_shapes=[rows, sums, cols] + stream,
        cost_estimate=matrix_cost, compiler_params=params(36), name="back_t",
    )(t_source, back_all)
    inner_all = exchange(third, BOTH)
    image_shape = (dp_size, wide + 8, LANES)
    fourth = pl.pallas_call(
        back_a, out_shape=shape(image_shape, f32),
        in_specs=[anywhere, in_vmem, in_vmem], out_specs=in_vmem, scratch_shapes=[rows, sums, cols] + stream,
        cost_estimate=matrix_cost, compiler_params=params(36), name="back_a",
    )(a_source, inner_all, solved)
    image_all = exchange(fourth, "dp")
    vec = shape((wide, LANES), f32)
    new_solution, new_residual, norm = pl.pallas_call(
        update, out_shape=(vec, vec, shape((centre_size, 8, LANES), f32)), compiler_params=params(8), name="update",
    )(image_all, rr, solution.reshape(wide, LANES), residual.reshape(wide, LANES), direction_rows)
    norms = exchange(norm, "centre")
    new_direction = pl.pallas_call(
        finish, out_shape=vec, compiler_params=params(8), name="finish",
    )(norms, rr, new_residual, direction_rows)
    return new_solution.reshape(-1), new_residual.reshape(-1), new_direction.reshape(-1)


def solution(mesh):
    placed = (
        P(None, "dp"),
        P(None, "centre"),
        P("dp", "centre"),
        P("dp", "centre"),
        P("centre"),
        P("centre"),
        P("centre"),
    )
    return jax.shard_map(
        body,
        mesh=mesh,
        in_specs=placed,
        out_specs=(P("centre"), P("centre"), P("centre")),
        check_vma=False,
    )
```

```python
import functools

import jax
import jax.numpy as jnp
from jax import lax
from jax.experimental import pallas as pl
from jax.experimental.pallas import tpu as pltpu
from jax.sharding import PartitionSpec as P

ridge_weight = 0.1
log2_e = 1.4426950408889634
LANES = 128
DEPTH = 64
PART = 256
PAIR = 1024
HEAD = 128
MIB = 1024 * 1024
BOTH = ("dp", "centre")


def params(mib):
    return pltpu.CompilerParams(vmem_limit_bytes=mib * MIB)


def whole(shape):
    return pl.BlockSpec(shape, lambda *_: (0,) * len(shape))


def row_product(tile_ref, vec_ref):
    total = None
    for k in range(vec_ref.shape[0]):
        term = tile_ref[:, k * LANES:(k + 1) * LANES] * vec_ref[k:k + 1, :]
        total = term if total is None else total + term
    return jnp.sum(total.T, axis=0, keepdims=True)


def write_all(out_ref, rows_ref, token_ref):
    token_ref[...] = jnp.zeros_like(token_ref)
    for place in range(out_ref.shape[0]):
        out_ref[place] = rows_ref[...]


def load_head(matrix_ref, after_ref, out_ref, sem):
    del after_ref
    copy = pltpu.make_async_copy(matrix_ref.at[pl.ds(0, out_ref.shape[0]), :], out_ref, sem)
    copy.start()
    copy.wait()


def start_stream(matrix_ref, held_ref, sems, begin=0):
    copies = [None] * begin
    for i in range(begin, matrix_ref.shape[0] // LANES):
        rows = pl.ds(i * LANES, LANES)
        copies.append(pltpu.make_async_copy(matrix_ref.at[rows, :], held_ref.at[rows, :], sems.at[i]))
        copies[-1].start()
    return copies


def stream_rows(copies, held_ref, vec_ref, rows_ref, out_ref, token_ref, head_ref=None):
    for i, copy in enumerate(copies):
        if copy is not None:
            copy.wait()
        source = head_ref if copy is None else held_ref
        rows_ref[i:i + 1, :] = row_product(source.at[i * LANES:(i + 1) * LANES, :], vec_ref)
    write_all(out_ref, rows_ref, token_ref)


def forward_direction(matrix_ref, vec_ref, out_ref, token_ref, rows_ref, held_ref, sems):
    stream_rows(start_stream(matrix_ref, held_ref, sems), held_ref, vec_ref, rows_ref, out_ref, token_ref)


def forward_gathered(centre_size, matrix_ref, head_ref, gathered_ref, out_ref, token_ref, rows_ref, vec_ref, held_ref, sems):
    copies = start_stream(matrix_ref, held_ref, sems, head_ref.shape[0] // LANES)
    deep = rows_ref.shape[0]
    blocks = vec_ref.shape[0] // deep
    first = lax.axis_index("centre") * blocks
    for i in range(blocks):
        part = gathered_ref[pl.ds((first + i) * centre_size, centre_size)]
        vec_ref[i * deep:(i + 1) * deep, :] = jnp.sum(part, axis=0)
    stream_rows(copies, held_ref, vec_ref, rows_ref, out_ref, token_ref, head_ref)


def column_of(row):
    return jnp.broadcast_to(row, (LANES, LANES)).T


def column_sums(copies, held_ref, vec_ref, sums_ref, whole_ref):
    sums_ref[...] = jnp.zeros_like(sums_ref)
    for i, copy in enumerate(copies):
        spread = column_of(vec_ref[i:i + 1, :])
        copy.wait()
        for k in range(held_ref.shape[1] // LANES):
            product = held_ref[i * LANES:(i + 1) * LANES, k * LANES:(k + 1) * LANES] * spread
            sums_ref[:, k * LANES:(k + 1) * LANES] += jnp.sum(product.reshape(LANES // 8, 8, LANES), axis=0)
    for k in range(whole_ref.shape[0]):
        whole_ref[k:k + 1, :] = jnp.sum(sums_ref[:, k * LANES:(k + 1) * LANES], axis=0, keepdims=True)


def back_t(scale, matrix_ref, gathered_ref, out_ref, vec_ref, sums_ref, whole_ref, held_ref, sems):
    copies = start_stream(matrix_ref, held_ref, sems)
    vec_ref[...] = jnp.sum(gathered_ref[...], axis=0) * scale
    column_sums(copies, held_ref, vec_ref, sums_ref, whole_ref)
    deep = vec_ref.shape[0]
    blocks = whole_ref.shape[0] // deep
    per = out_ref.shape[0] // lax.axis_size("dp")
    for place in range(out_ref.shape[0]):
        half = (place // per) % blocks
        out_ref[place] = whole_ref[half * deep:(half + 1) * deep, :]


def back_a(matrix_ref, gathered_ref, solved_ref, out_ref, vec_ref, sums_ref, whole_ref, held_ref, sems):
    copies = start_stream(matrix_ref, held_ref, sems)
    deep = vec_ref.shape[0]
    dp_size = lax.axis_size("dp")
    centre_size = lax.axis_size("centre")
    blocks = whole_ref.shape[0] // deep
    place = lax.axis_index("dp")
    source = place // blocks
    solved = jnp.sum(solved_ref[pl.ds(place * centre_size, centre_size)], axis=0)
    total = gathered_ref[source]
    for p in range(1, dp_size):
        total = total + gathered_ref[p * centre_size + source]
    inner = total + ridge_weight * solved
    vec_ref[...] = inner
    dot = jnp.full((8, LANES), jnp.sum(inner * solved), jnp.float32)
    column_sums(copies, held_ref, vec_ref, sums_ref, whole_ref)
    size = whole_ref.shape[0]
    for place in range(out_ref.shape[0]):
        out_ref[place, :size, :] = whole_ref[...]
        out_ref[place, size:, :] = dot


def rounded(values):
    return values.astype(jnp.bfloat16).astype(jnp.float32)


def three(values):
    first = rounded(values)
    rest = values - first
    second = rounded(rest)
    return first, second, rounded(rest - second)


def store_splits(target_ref, start, values, norms, order, norm_first):
    width = values.shape[1]
    pieces = three(values)
    norm_rows = list(three(norms))
    ones = [jnp.ones_like(norms)] * 3
    last = [pieces[i][8:9] for i in order] + (norm_rows + ones if norm_first else ones + norm_rows)
    tail = jnp.concatenate(last + [jnp.zeros((4, width), jnp.float32)], axis=0)
    groups = [pieces[i][:8] for i in order] + [tail[:8], tail[8:]]
    for row in range(0, len(groups), 2):
        pair = jnp.concatenate(groups[row:row + 2], axis=0)
        target_ref[row * 8:row * 8 + 16, pl.ds(start, width)] = pair.astype(target_ref.dtype)


def half_start(width, other):
    return pl.multiple_of(lax.rem(lax.axis_index("dp") + other, 2) * width, LANES)


def lay_out(centres, residual, block):
    share = centres.shape[1]
    part = share // 4
    block[:, :share] = centres[:8, :]
    for s in range(4):
        block[s:s + 1, share:] = centres[8:9, s * part:(s + 1) * part]
        block[4 + s:5 + s, share:] = residual[:, s * part:(s + 1) * part]


def pack(centres_ref, residual_ref, after_ref, half_ref, own):
    del after_ref
    lay_out(centres_ref, residual_ref, own)
    width = half_ref.shape[1]
    half_ref[...] = own[:, pl.ds(half_start(width, 0), width)]


def operands(feat, steps, points_ref, centres_ref, residual_ref, *refs):
    halves, refs = refs[:2 * steps], refs[2 * steps:]
    after_ref, x_ref, c_ref, rr_ref, rows_x, points_v, centres_v, residual_v, pieces, sems = refs
    del after_ref
    centre_size = lax.axis_size("centre")
    here = lax.axis_index("centre")
    mine = x_ref.shape[0]
    share = c_ref.shape[1] // centre_size
    part = share // 4
    width = halves[0].shape[1]
    start = pl.multiple_of(here * mine, LANES)
    copies = [
        pltpu.make_async_copy(points_ref.at[:, pl.ds(start, mine)], points_v, sems.at[0]),
        pltpu.make_async_copy(centres_ref, centres_v, sems.at[1]),
        pltpu.make_async_copy(residual_ref, residual_v, sems.at[2]),
    ]
    for i, half in enumerate(halves):
        place = pieces.at[1 + i % steps, :, pl.ds(half_start(width, i // steps), width)]
        copies.append(pltpu.make_async_copy(half, place, sems.at[3 + i]))
    for copy in copies:
        copy.start()
    for copy in copies:
        copy.wait()
    lay_out(centres_v, residual_v, pieces.at[0])
    scale = log2_e / feat
    x = points_v[...]
    norms = -scale * jnp.sum(x * x, axis=0, keepdims=True)
    store_splits(rows_x, 0, x, norms, (0, 0, 1, 1, 0, 2), True)
    for r in range(mine // LANES):
        x_ref[r * LANES:(r + 1) * LANES, :] = rows_x[:, r * LANES:(r + 1) * LANES].T.astype(jnp.bfloat16)
    rr = jnp.zeros((1, 1), jnp.float32)
    for back_by in range(steps + 1):
        place = lax.rem(here + centre_size - back_by, centre_size)
        start = pl.multiple_of(place * share, LANES)
        for s in range(4):
            c = jnp.concatenate([pieces[back_by, :, s * part:(s + 1) * part], pieces[back_by, s:s + 1, share:]], axis=0)
            norms = -scale * jnp.sum(c * c, axis=0, keepdims=True)
            at = pl.multiple_of(start + s * part, LANES)
            store_splits(c_ref, at, c * (2.0 * scale), norms, (0, 1, 0, 1, 2, 0), False)
            res = pieces[back_by, 4 + s:5 + s, share:]
            rr = rr + jnp.sum(res * res, axis=1, keepdims=True)
    rr_ref[...] = jnp.broadcast_to(rr, rr_ref.shape)


def kernel_products(block, chunk, x_ref, c_ref, gathered_ref, out_ref, w_ref, tile_ref, fit_ref, f_ref, back_ref):
    centre_size = lax.axis_size("centre")
    dp_size = lax.axis_size("dp")
    deep = gathered_ref.shape[1]
    width = chunk // LANES
    chunks = c_ref.shape[1] // chunk
    for p in range(dp_size):
        w_ref[p * deep:(p + 1) * deep, :] = jnp.sum(gathered_ref[p * centre_size:(p + 1) * centre_size], axis=0)
    back_ref[...] = jnp.zeros_like(back_ref)
    f_ref[...] = jnp.zeros_like(f_ref)

    def points_block(step, carry):
        fit_ref[...] = jnp.zeros_like(fit_ref)

        def first_pass(n, carry):
            at = pl.multiple_of(n * chunk, chunk)
            c = c_ref[:, pl.ds(at, chunk)]
            for r in range(0, block, PART):
                x = x_ref[pl.ds(pl.multiple_of(step * block + r, PART), PART), :]
                power = jnp.dot(x, c, preferred_element_type=jnp.float32)
                value = jnp.exp2(power)
                tile_ref[r:r + PART, pl.ds(at, chunk)] = value.astype(jnp.bfloat16)
                total = fit_ref[r:r + PART, :]
                for k in range(width):
                    total = total + value[:, k * LANES:(k + 1) * LANES] * w_ref[pl.ds(n * width + k, 1), :]
                fit_ref[r:r + PART, :] = total
            return carry

        lax.fori_loop(0, chunks, first_pass, 0, unroll=16)
        for r in range(0, block, LANES):
            f = jnp.sum(fit_ref[r:r + LANES, :].T, axis=0, keepdims=True)
            first = rounded(f)
            rows = jnp.concatenate([first, f - first, jnp.zeros((14, LANES), jnp.float32)], axis=0)
            f_ref[:, r:r + LANES] = rows.astype(jnp.bfloat16)

        def second_pass(n, carry):
            at = pl.multiple_of(n * PAIR, PAIR)
            back_ref[:, pl.ds(at, PAIR)] += jnp.dot(
                f_ref[...], tile_ref[:, pl.ds(at, PAIR)], preferred_element_type=jnp.float32
            )
            return carry

        lax.fori_loop(0, c_ref.shape[1] // PAIR, second_pass, 0, unroll=16)
        return carry

    lax.fori_loop(0, x_ref.shape[0] // block, points_block, 0)
    for p in range(dp_size):
        for k in range(deep):
            at = (p * deep + k) * LANES
            row = back_ref[0:1, at:at + LANES] + back_ref[1:2, at:at + LANES]
            for c in range(centre_size):
                out_ref[p * centre_size + c, k:k + 1, :] = row


def update(gathered_ref, rr_ref, solution_ref, residual_ref, direction_ref, new_solution_ref, new_residual_ref, kept_ref, norm_ref):
    size = solution_ref.shape[0]
    total = jnp.sum(gathered_ref[...], axis=0)
    alpha = rr_ref[0:1, 0:1] / total[size:size + 1, 0:1]
    new_solution_ref[...] = solution_ref[...] + alpha * direction_ref[...]
    new_residual = residual_ref[...] - alpha * total[:size]
    new_residual_ref[...] = new_residual
    kept_ref[...] = new_residual
    norm_ref[...] = jnp.full(norm_ref.shape, jnp.sum(new_residual * new_residual), jnp.float32)


def finish(norms_ref, rr_ref, new_residual_ref, direction_ref, out_ref):
    norm_new = jnp.sum(norms_ref[...], axis=0)[0:1, 0:1]
    out_ref[...] = new_residual_ref[...] + (norm_new / rr_ref[0:1, 0:1]) * direction_ref[...]


def body(points, centres, t_inverse, a_inverse, solution, residual, direction):
    f32 = jnp.float32
    rows_block, cols_block = t_inverse.shape
    feat = points.shape[0]
    dp_size = lax.axis_size("dp")
    centre_size = lax.axis_size("centre")
    devices = dp_size * centre_size
    deep = rows_block // LANES
    wide = cols_block // LANES
    count = points.shape[1] * dp_size
    mine = points.shape[1] // centre_size
    total = cols_block * centre_size
    shape = jax.ShapeDtypeStruct
    spread_shape = (devices, deep, LANES)
    sums = pltpu.VMEM((8, cols_block), f32)

    in_vmem = pl.BlockSpec(memory_space=pltpu.VMEM)
    anywhere = pl.BlockSpec(memory_space=pl.ANY)
    matrix_bytes = rows_block * cols_block * 4
    matrix_cost = pl.CostEstimate(flops=2 * rows_block * cols_block, bytes_accessed=matrix_bytes, transcendentals=0)

    def exchange(values, axes):
        return lax.all_to_all(values, axes, 0, 0, tiled=True)

    stream = [pltpu.VMEM((rows_block, cols_block), f32), pltpu.SemaphoreType.DMA((deep,))]
    rows = pltpu.VMEM((deep, LANES), f32)
    cols = pltpu.VMEM((wide, LANES), f32)
    a_source = pltpu.with_memory_space_constraint(a_inverse, pltpu.HBM)
    t_source = pltpu.with_memory_space_constraint(t_inverse, pltpu.HBM)

    def load(source, after):
        head = pl.pallas_call(
            load_head, out_shape=pltpu.VMEM((HEAD, cols_block), f32), in_specs=[anywhere] * 2, out_specs=in_vmem,
            scratch_shapes=[pltpu.SemaphoreType.DMA], cost_estimate=pl.CostEstimate(
                flops=0, bytes_accessed=4 * HEAD * cols_block, transcendentals=0,
            ),
            compiler_params=params(4), name="load",
        )(source, after)
        return pltpu.with_memory_space_constraint(head, pltpu.VMEM)

    direction_rows = direction.reshape(wide, LANES)
    token = shape((8, LANES), f32)
    first, first_done = pl.pallas_call(
        forward_direction, out_shape=(shape(spread_shape, f32), token),
        in_specs=[anywhere, in_vmem], out_specs=(in_vmem,) * 2, scratch_shapes=[rows] + stream,
        cost_estimate=matrix_cost, compiler_params=params(36), name="solve_a",
    )(a_source, direction_rows)
    packed = cols_block + cols_block // 4
    residual_row = residual.reshape(1, cols_block)
    half = pl.pallas_call(
        pack, out_shape=shape((8, packed // 2), f32), in_specs=[in_vmem, in_vmem, anywhere], out_specs=in_vmem,
        scratch_shapes=[pltpu.VMEM((8, packed), f32)], compiler_params=params(4), name="pack",
    )(centres, residual_row, first_done)
    steps = centre_size - 1
    moved = [
        lax.ppermute(half, "centre", [(i, (i + by) % centre_size) for i in range(centre_size)])
        for by in range(1, centre_size)
    ]
    solved = exchange(first, BOTH)
    second, second_done = pl.pallas_call(
        functools.partial(forward_gathered, centre_size), out_shape=(shape(spread_shape, f32), token),
        in_specs=[anywhere, in_vmem, in_vmem], out_specs=(in_vmem,) * 2, scratch_shapes=[rows, cols] + stream,
        cost_estimate=matrix_cost, compiler_params=params(36), name="solve_t",
    )(t_source, load(t_source, first_done), solved)
    second, moved = lax.optimization_barrier((second, moved))
    weights = exchange(second, BOTH)
    swapped = [lax.ppermute(piece, "dp", [(i, i ^ 1) for i in range(dp_size)]) for piece in moved]
    block, chunk = min(1024, mine), 256
    sources = [pltpu.with_memory_space_constraint(v, pltpu.HBM) for v in [points, centres, residual_row] + list(moved) + swapped]
    x_rows, c_rows, rr = pl.pallas_call(
        functools.partial(operands, feat, steps),
        out_shape=(shape((mine, DEPTH), jnp.bfloat16), shape((DEPTH, total), jnp.bfloat16), shape((8, LANES), f32)),
        in_specs=[anywhere] * (4 + 2 * steps), out_specs=(in_vmem,) * 3,
        scratch_shapes=[
            pltpu.VMEM((DEPTH, mine), f32), pltpu.VMEM((feat, mine), f32),
            pltpu.VMEM((feat, cols_block), f32), pltpu.VMEM((1, cols_block), f32),
            pltpu.VMEM((steps + 1, 8, packed), f32), pltpu.SemaphoreType.DMA((3 + 2 * steps,)),
        ],
        compiler_params=params(12), name="operands",
    )(*sources, second_done)
    back = pl.pallas_call(
        functools.partial(kernel_products, block, chunk), out_shape=shape(spread_shape, f32),
        in_specs=[in_vmem] * 3, out_specs=in_vmem,
        scratch_shapes=[
            pltpu.VMEM((total // LANES, LANES), f32),
            pltpu.VMEM((block, total), jnp.bfloat16),
            pltpu.VMEM((block, LANES), f32),
            pltpu.VMEM((16, block), jnp.bfloat16),
            pltpu.VMEM((16, total), f32),
        ],
        compiler_params=params(42), name="kernel_pair",
    )(x_rows, c_rows, weights)
    back_all = exchange(back, BOTH)
    third = pl.pallas_call(
        functools.partial(back_t, 1.0 / count), out_shape=shape(spread_shape, f32),
        in_specs=[anywhere, in_vmem], out_specs=in_vmem, scratch_shapes=[rows, sums, cols] + stream,
        cost_estimate=matrix_cost, compiler_params=params(36), name="back_t",
    )(t_source, back_all)
    inner_all = exchange(third, BOTH)
    image_shape = (dp_size, wide + 8, LANES)
    fourth = pl.pallas_call(
        back_a, out_shape=shape(image_shape, f32),
        in_specs=[anywhere, in_vmem, in_vmem], out_specs=in_vmem, scratch_shapes=[rows, sums, cols] + stream,
        cost_estimate=matrix_cost, compiler_params=params(36), name="back_a",
    )(a_source, inner_all, solved)
    image_all = exchange(fourth, "dp")
    vec = shape((wide, LANES), f32)
    new_solution, new_residual, kept, norm = pl.pallas_call(
        update, out_shape=(vec, vec, vec, shape((centre_size, 8, LANES), f32)), compiler_params=params(8), name="update",
    )(image_all, rr, solution.reshape(wide, LANES), residual.reshape(wide, LANES), direction_rows)
    norms = exchange(norm, "centre")
    new_direction = pl.pallas_call(
        finish, out_shape=vec, compiler_params=params(8), name="finish",
    )(norms, rr, kept, direction_rows)
    return new_solution.reshape(-1), new_residual.reshape(-1), new_direction.reshape(-1)


def solution(mesh):
    placed = (
        P(None, "dp"),
        P(None, "centre"),
        P("dp", "centre"),
        P("dp", "centre"),
        P("centre"),
        P("centre"),
        P("centre"),
    )
    return jax.shard_map(
        body,
        mesh=mesh,
        in_specs=placed,
        out_specs=(P("centre"), P("centre"), P("centre")),
        check_vma=False,
    )
```
